512 devices in a mesh: section: 4 (over y), vocab: 32 (over x, z_hi, core), rep: 4 (over z_lo).
Axes of the slice: x: 4, y: 4, z: 16 (z_hi: 4, z_lo: 4; z = z_hi * 4 + z_lo), core: 2. Of those that a mesh axis runs over, the one named last changes fastest.
Arguments:
- hidden: bfloat16 [384, 8192], P(('vocab', 'rep'), 'section'), may hold values from -6 to 6
- head_weight: bfloat16 [8192, 65536], P('section', ('vocab', 'rep')), may hold values from -0.20992233 to 0.20992233
- targets: int32 [384], replicated, may hold values from 0 to 65535
Outputs:
- d_hidden: bfloat16 [384, 8192], P(('vocab', 'rep'), 'section')
- d_head: bfloat16 [8192, 65536], P('section', ('vocab', 'rep'))
- loss: float32 [2], replicated
The draws below stay inside these ranges and needn't reach their ends.
All inputs are finite; a program needn't handle non-finite values.
Results may differ from the reference program's by a relative error of at most 0.013.
Values may be sent and summed in bfloat16 or wider, within the bound.
A program may use at most 64 MiB of HBM per device.

```python
import math
import jax
import jax.numpy as jnp
import numpy as np
from jax import lax

D = 8192
V = 65536
MICRO = 2
MB_TOK = 192
TOKENS = 384


def shared_direction(key):
    coin_flips = jax.random.bernoulli(jax.random.fold_in(key, 101), 0.5, (D,))
    return jnp.where(coin_flips, 1.0, -1.0).astype(jnp.float32)


def shared_columns(key):
    first_col = jax.random.randint(jax.random.fold_in(key, 102), (), 0, V)
    return first_col


def drawn_row(key):
    return jax.random.randint(jax.random.fold_in(key, 103), (), 0, TOKENS)


def draw_hidden(key, part):
    direction = shared_direction(key)
    chosen_row = drawn_row(key)
    key = jax.random.fold_in(key, 7)
    key_one = jax.random.fold_in(key, 0)
    result = jnp.clip(jax.random.normal(key_one, (TOKENS, D), jnp.float32), -6.0, 6.0)
    rows = jnp.arange(TOKENS, dtype=jnp.int32)
    result = jnp.where(rows[:, None] == chosen_row, 0.6 * direction[None, :], result)
    return result.astype(jnp.bfloat16)


def draw_head_weight(key, part):
    direction = shared_direction(key)
    first_col = shared_columns(key)
    key = jax.random.fold_in(key, 11)
    key_one = jax.random.fold_in(key, 0)
    magnitude = 3.0 / jnp.sqrt(jnp.float32(D))
    columns = jnp.arange(V, dtype=jnp.int32)
    result = jnp.clip(jax.random.normal(key_one, (D, V), jnp.float32), -6.0, 6.0) * magnitude
    planted = direction[:, None] * (3.2 / jnp.sqrt(jnp.float32(D)))
    result = jnp.where(columns[None, :] == first_col, planted, result)
    return result.astype(jnp.bfloat16)


def touch_ends(array, key, smallest, top_value):
    place = [jax.random.randint(jax.random.fold_in(key, axis), (), 0, length) for axis, length in enumerate(array.shape)]
    main_axis = array.shape.index(max(array.shape))
    neighbour = place[:main_axis] + [(place[main_axis] + 1) % array.shape[main_axis]] + place[main_axis + 1:]
    return array.at[tuple(place)].set(smallest).at[tuple(neighbour)].set(top_value)


def rank_bounds(number_of, skew):
    loads = [(1 << 20) // math.isqrt(standing ** skew) + 1 for standing in range(1, number_of + 1)]
    deviation = 1 + sum(loads) // (1 << 30)
    return np.cumsum(np.array([max(1, weight // deviation) for weight in loads]))


def ranked_ids(own_key, extent, amount, lean):
    table = rank_bounds(amount, lean)
    ticket = jax.random.randint(jax.random.fold_in(own_key, 1), extent, 0, int(table[amount - 1]))
    standing = jnp.searchsorted(jnp.asarray(table, jnp.int32), ticket, side="right")
    return jax.random.permutation(jax.random.fold_in(own_key, 2), amount)[standing].astype(jnp.int32)


def setup_inputs(seed: int = 0) -> dict:
    seeds = jax.random.split(jax.random.key(seed), 4)
    hidden = draw_hidden(jax.random.fold_in(seeds[3], 71), 0)
    head_weight = draw_head_weight(jax.random.fold_in(seeds[3], 71), 0)
    targets = touch_ends(ranked_ids(seeds[2], (TOKENS,), V, 2), jax.random.fold_in(seeds[2], 3), 0, V - 1).astype(jnp.int32)
    return {"hidden": hidden, "head_weight": head_weight, "targets": targets}


z_weight = 0.01


def reference(hidden, head_weight, targets):
    logits = jnp.dot(hidden, head_weight, preferred_element_type=jnp.float32)
    row_top = jnp.max(logits, axis=1)
    row_total = jnp.sum(jnp.exp(logits - row_top[:, None]), axis=1)
    log_total = row_top + jnp.log(row_total)
    columns = jnp.arange(V, dtype=jnp.int32)
    is_target = columns[None, :] == targets.astype(jnp.int32)[:, None]
    picked = jnp.sum(jnp.where(is_target, logits, 0.0), axis=1)
    row_loss = log_total - picked + z_weight * log_total * log_total
    micro_index = jnp.arange(TOKENS, dtype=jnp.int32) // MB_TOK
    member = micro_index[None, :] == jnp.arange(MICRO, dtype=jnp.int32)[:, None]
    loss = jnp.sum(jnp.where(member, row_loss[None, :], 0.0), axis=1) / MB_TOK
    softmax = jnp.exp(logits - log_total[:, None])
    grads = (softmax * (1.0 + 2.0 * z_weight * log_total)[:, None] - is_target.astype(jnp.float32)).astype(jnp.bfloat16)
    d_hidden = lax.dot_general(grads, head_weight, (((1,), (1,)), ((), ())), preferred_element_type=jnp.float32).astype(jnp.bfloat16)
    d_head = lax.dot_general(hidden, grads, (((0,), (0,)), ((), ())), preferred_element_type=jnp.float32).astype(jnp.bfloat16)
    return (d_hidden, d_head, loss)
```

```python
import jax
import jax.numpy as jnp
from jax import lax
from jax.experimental import pallas as pl
from jax.experimental.pallas import tpu as pltpu
from jax.sharding import PartitionSpec as P

MESH = pl.DeviceIdType.MESH
F32, BF16 = jnp.float32, jnp.bfloat16
Z_WEIGHT = 0.01
MB_TOK = 192


def swap_matrix():
    row = lax.broadcasted_iota(jnp.int32, (256, 256), 0)
    col = lax.broadcasted_iota(jnp.int32, (256, 256), 1)
    return jnp.where(col == (row % 16) * 16 + row // 16, 1.0, 0.0).astype(BF16)


def merge(tiles):
    top = jnp.max(tiles[:, 0:1, :], axis=0)
    total = jnp.sum(tiles[:, 1:2, :] * jnp.exp(tiles[:, 0:1, :] - top[None]), axis=0)
    picked = jnp.sum(tiles[:, 2:3, :], axis=0)
    return top, total, picked


def as_tile(top, total, picked):
    row = lax.broadcasted_iota(jnp.int32, (8, 128), 0)
    return jnp.where(row == 0, top, jnp.where(row == 1, total, picked))


def kernel(
    hid, w_hbm, tgt, dh_out, dw_hbm, loss_out,
    w, gat, xs, lp, rb, lown, sta, stb, stc, gs, gb, pf, cs, cr, xsnd, xr, un, zs, za, zb, zsum, zq, zr, lo, dw, pk,
    ss, rs, local,
):
    y = lax.axis_index("section")
    v = lax.axis_index("vocab")
    zl = lax.axis_index("rep")
    c = lax.rem(v, 2)
    zh = lax.rem(lax.div(v, 2), 4)
    x = lax.div(v, 8)
    z = zh * 4 + zl
    slot = zl * 4 + zh
    other = 1 - c

    def at(x=x, y=y, z=z, c=c):
        x, y, z = lax.rem(x + 4, 4), lax.rem(y + 4, 4), lax.rem(z + 16, 16)
        return (y, (x * 4 + lax.div(z, 4)) * 2 + c, lax.rem(z, 4))

    copies = []

    def send(src, dst, dest):
        k = len(copies)
        copy = pltpu.make_async_remote_copy(
            src, dst, ss.at[k], rs.at[k], device_id=dest, device_id_type=MESH
        )
        copy.start()
        copies.append(copy)
        return copy

    w_copy = pltpu.make_async_copy(w_hbm, w, local.at[0])
    w_copy.start()

    def mate(k):
        n = lax.rem(x * 2 + c + k, 8)
        return at(x=lax.div(n, 2), c=lax.rem(n, 2))

    def quad(k):
        return at(z=zh * 4 + lax.rem(zl + k, 4))

    partners = (
        [at(z=z + 4 * k) for k in (2, 1, 3)]
        + [at(z=z + k) for k in (2, -2, 1, -1)]
        + [quad(k) for k in (1, 2, 3)]
        + [mate(k) for k in range(1, 8)]
        + [at(y=y + k) for k in (1, 2, 3)]
    )
    barrier = pltpu.get_barrier_semaphore()
    for p in partners:
        pl.semaphore_signal(barrier, inc=1, device_id=p, device_id_type=MESH)
    h = hid[...].astype(F32)
    for i in range(3):
        for j in range(16):
            pk[j : j + 1, i * 128 : (i + 1) * 128] = h[i : i + 1, j * 128 : (j + 1) * 128]
    gat[slot] = pk[...].astype(BF16)
    pl.semaphore_wait(barrier, len(partners))

    first = [send(gat.at[slot], gat.at[slot], at(z=z + 4 * k)) for k in (2, 1, 3)]
    for t in first:
        t.wait_recv()
    own_set = gat.at[pl.ds(zl * 4, 4)]
    low, high = gat.at[pl.ds(zl * 4, 2)], gat.at[pl.ds(zl * 4 + 2, 2)]
    second = [
        send(low, low, at(z=z + 2)),
        send(high, high, at(z=z - 2)),
        send(own_set, own_set, at(z=z + 1)),
        send(own_set, own_set, at(z=z - 1)),
    ]
    swap = swap_matrix()
    for t in second:
        t.wait_recv()
    turned = jnp.dot(swap, gat[...].reshape(256, 384), preferred_element_type=F32).astype(BF16)
    mine = x * 2 + c
    for i in range(3):
        for j in range(16):
            xs[mine, i * 16 : (i + 1) * 16, j * 128 : (j + 1) * 128] = turned[
                j * 16 : (j + 1) * 16, i * 128 : (i + 1) * 128
            ]

    over_x = {k: send(xs.at[mine], xs.at[mine], at(x=x + k)) for k in (2, 1, 3)}
    sib = {0: send(xs.at[mine], xs.at[mine], at(c=other))}
    w_copy.wait()

    def slab_from(k):
        return lax.rem(x - k + 4, 4)

    def hand_on(k):
        over_x[k].wait_recv()
        group = xs.at[slab_from(k) * 2 + c]
        sib[k] = send(group, group, at(c=other))

    ks = (0, 1, 3, 2)
    over_y = []

    def slab_logits(d):
        sib[ks[d]].wait_recv()
        rows = xs[pl.ds(slab_from(ks[d]) * 2, 2)].reshape(96, 2048)
        lp[d] = jnp.dot(rows, w[...], preferred_element_type=F32)
        for t in (2, 1, 3):
            to = lax.rem(y + t, 4)
            over_y.append(send(lp.at[d, pl.ds(to * 24, 24)], rb.at[t - 1, d], at(y=y + t)))

    slab_logits(0)
    hand_on(1)
    hand_on(3)
    slab_logits(1)
    slab_logits(2)
    hand_on(2)
    slab_logits(3)
    for t in over_y:
        t.wait_recv()
    for d in range(4):
        own = lp[d, pl.ds(pl.multiple_of(y * 24, 8), 24), :]
        lown[slab_from(ks[d])] = (own + rb[0, d]) + (rb[1, d] + rb[2, d])

    logits = lown[...].reshape(96, 512)
    first_col = (v * 4 + zl) * 512
    targets = tgt[:, pl.ds(pl.multiple_of(y * 24, 8), 24), :].reshape(96, 1)
    is_target = lax.broadcasted_iota(jnp.int32, (96, 512), 1) + first_col == targets
    own_top = jnp.max(logits, axis=1, keepdims=True)
    own_total = jnp.sum(jnp.exp(logits - own_top), axis=1, keepdims=True)
    own_pick = jnp.sum(jnp.where(is_target, logits, 0.0), axis=1, keepdims=True)
    lane = lax.broadcasted_iota(jnp.int32, (96, 128), 1)
    cols = jnp.where(lane == 0, own_top, jnp.where(lane == 1, own_total, own_pick))
    cols = jnp.concatenate([cols, jnp.ones((32, 128), F32)], axis=0)
    sta[x * 2 + c] = cols.T[:8]
    moves = [send(sta.at[x * 2 + c], sta.at[x * 2 + c], mate(k)) for k in range(1, 8)]
    for t in moves:
        t.wait_recv()
    stb[zl] = as_tile(*merge(sta[...]))
    moves = [send(stb.at[zl], stb.at[zl], quad(k)) for k in (1, 2, 3)]
    for t in moves:
        t.wait_recv()
    stc[zh] = as_tile(*merge(stb[...]))
    moves = [send(stc.at[zh], stc.at[zh], at(z=z + 4 * k)) for k in (2, 1, 3)]
    for t in moves:
        t.wait_recv()
    top, total, picked = merge(stc[...])
    log_total = top + jnp.log(total)

    lt = jnp.broadcast_to(log_total, (128, 128)).T[:96, 0:1]
    grads = jnp.exp(logits - lt) * (1.0 + 2.0 * Z_WEIGHT * lt) - is_target.astype(F32)
    gs[y] = grads.astype(BF16)
    over_y = [send(gs.at[y], gs.at[y], at(y=y + t)) for t in (2, 1, 3)]

    row_loss = log_total - picked + Z_WEIGHT * log_total * log_total
    lane = lax.broadcasted_iota(jnp.int32, (1, 128), 1)
    loss0 = jnp.sum(jnp.where(lane < 48, row_loss, 0.0), axis=1, keepdims=True) / MB_TOK
    loss1 = jnp.sum(jnp.where((lane >= 48) & (lane < 96), row_loss, 0.0), axis=1, keepdims=True) / MB_TOK
    lo[y] = jnp.broadcast_to(jnp.where(lane == 0, loss0, loss1), (8, 128))
    losses = [send(lo.at[y], lo.at[y], at(y=y + t)) for t in (2, 1, 3)]

    for t in over_y:
        t.wait_recv()
    shares = [gs[s].astype(F32) for s in range(4)]
    for k in range(4):
        gb[k] = jnp.concatenate([g[k * 24 : (k + 1) * 24] for g in shares], axis=0).astype(BF16)

    ks = (2, 1, 3, 0)
    over_c = []
    for d, k in enumerate(ks):
        part = lax.dot_general(
            gb[lax.rem(x + k, 4)], w[...], (((1,), (1,)), ((), ())), preferred_element_type=F32
        )
        pf[d] = part.reshape(2, 48, 2048)
        cs[d] = pf[d, other].astype(BF16)
        over_c.append(send(cs.at[d], cr.at[d], at(c=other)))
    over_x = []
    for d, k in enumerate(ks):
        over_c[d].wait_recv()
        if k:
            xsnd[d] = (pf[d, c] + cr[d].astype(F32)).astype(BF16)
            over_x.append(send(xsnd.at[d], xr.at[d], at(x=x + k)))

    @pl.loop(0, 8)
    def _(n):
        cut = pl.ds(pl.multiple_of(n * 256, 256), 256)
        dw[cut, :] = lax.dot_general(
            xs[:, :, cut].reshape(384, 256), gb[...].reshape(384, 512), (((0,), (0,)), ((), ())),
            preferred_element_type=F32,
        ).astype(BF16)

    dw_copy = pltpu.make_async_copy(dw, dw_hbm, local.at[1])
    dw_copy.start()

    for t in over_x:
        t.wait_recv()
    acc = pf[3, c] + cr[3].astype(F32)
    for d in range(3):
        acc = acc + xr[d].astype(F32)
    acc = acc.astype(BF16)
    for i in range(3):
        for j in range(16):
            un[j * 16 : (j + 1) * 16, i * 128 : (i + 1) * 128] = acc[
                i * 16 : (i + 1) * 16, j * 128 : (j + 1) * 128
            ]
    zs[...] = jnp.dot(swap, un[...], preferred_element_type=F32).astype(BF16).reshape(16, 16, 384)

    far = lax.rem(zl + 2, 4) * 4
    moves = [
        send(zs.at[pl.ds(far, 2)], zb.at[0], at(z=z - 2)),
        send(zs.at[pl.ds(far + 2, 2)], zb.at[1], at(z=z + 2)),
        send(zs.at[pl.ds(lax.rem(zl + 1, 4) * 4, 4)], za.at[0], at(z=z + 1)),
        send(zs.at[pl.ds(lax.rem(zl + 3, 4) * 4, 4)], za.at[1], at(z=z - 1)),
    ]
    for t in moves:
        t.wait_recv()
    zsum[...] = (
        zs[pl.ds(zl * 4, 4)].astype(F32)
        + za[0].astype(F32)
        + za[1].astype(F32)
        + zb[...].reshape(4, 16, 384).astype(F32)
    )
    zq[...] = zsum[...].astype(BF16)
    moves = [send(zq.at[lax.rem(zh + k, 4)], zr.at[k - 1], at(z=z + 4 * k)) for k in (2, 1, 3)]
    for t in losses:
        t.wait_recv()
    loss_out[...] = (lo[0] + lo[1]) + (lo[2] + lo[3])
    for t in moves:
        t.wait_recv()
    pk[...] = zsum[zh] + zr[0].astype(F32) + zr[1].astype(F32) + zr[2].astype(F32)
    rows = []
    for i in range(3):
        rows.append(jnp.concatenate([pk[j : j + 1, i * 128 : (i + 1) * 128] for j in range(16)], axis=1))
    dh_out[...] = jnp.concatenate(rows, axis=0).astype(BF16)

    for t in copies:
        t.wait_send()
    dw_copy.wait()


N_COPIES = 3 + 4 + 3 + 4 + 12 + 13 + 3 + 3 + 4 + 3 + 4 + 3


def on_device(hidden, head_weight, targets):
    column = targets.reshape(4, 4, 2, 4, 3).transpose(0, 2, 4, 3, 1).reshape(4, 96, 1)
    vmem = pl.BlockSpec(memory_space=pltpu.VMEM)
    hbm = pl.BlockSpec(memory_space=pl.ANY)
    scratch = [
        ((2048, 512), BF16),
        ((16, 16, 384), BF16),
        ((8, 48, 2048), BF16),
        ((4, 96, 512), F32),
        ((3, 4, 24, 512), F32),
        ((4, 24, 512), F32),
        ((8, 8, 128), F32),
        ((4, 8, 128), F32),
        ((4, 8, 128), F32),
        ((4, 96, 512), BF16),
        ((4, 96, 512), BF16),
        ((4, 2, 48, 2048), F32),
        ((4, 48, 2048), BF16),
        ((4, 48, 2048), BF16),
        ((3, 48, 2048), BF16),
        ((3, 48, 2048), BF16),
        ((256, 384), BF16),
        ((16, 16, 384), BF16),
        ((2, 4, 16, 384), BF16),
        ((2, 2, 16, 384), BF16),
        ((4, 16, 384), F32),
        ((4, 16, 384), BF16),
        ((3, 16, 384), BF16),
        ((4, 8, 128), F32),
        ((2048, 512), BF16),
        ((16, 384), F32),
    ]
    d_hidden, d_head, loss = pl.pallas_call(
        kernel,
        out_shape=(
            jax.ShapeDtypeStruct((3, 2048), BF16),
            jax.ShapeDtypeStruct((2048, 512), BF16),
            jax.ShapeDtypeStruct((8, 128), F32),
        ),
        in_specs=[vmem, hbm, vmem],
        out_specs=(vmem, hbm, vmem),
        scratch_shapes=[pltpu.VMEM(s, t) for s, t in scratch]
        + [pltpu.SemaphoreType.DMA((N_COPIES,)), pltpu.SemaphoreType.DMA((N_COPIES,)), pltpu.SemaphoreType.DMA((2,))],
        compiler_params=pltpu.CompilerParams(
            collective_id=0, has_side_effects=True, vmem_limit_bytes=48 * 1024 * 1024
        ),
        name="head",
    )(hidden, head_weight, column)
    return d_hidden, d_head, loss[0, :2]


def solution(mesh):
    return jax.shard_map(
        on_device,
        mesh=mesh,
        in_specs=(P(("vocab", "rep"), "section"), P("section", ("vocab", "rep")), P()),
        out_specs=(P(("vocab", "rep"), "section"), P("section", ("vocab", "rep")), P()),
        check_vma=False,
    )
```

```python
import jax
import jax.numpy as jnp
from jax import lax
from jax.experimental import pallas as pl
from jax.experimental.pallas import tpu as pltpu
from jax.sharding import PartitionSpec as P

MESH = pl.DeviceIdType.MESH
F32, BF16 = jnp.float32, jnp.bfloat16
Z_WEIGHT = 0.01
MB_TOK = 192


def swap_matrix():
    row = lax.broadcasted_iota(jnp.int32, (256, 256), 0)
    col = lax.broadcasted_iota(jnp.int32, (256, 256), 1)
    return jnp.where(col == (row % 16) * 16 + row // 16, 1.0, 0.0).astype(BF16)


def merge(tiles):
    top = jnp.max(tiles[:, 0:1, :], axis=0)
    total = jnp.sum(tiles[:, 1:2, :] * jnp.exp(tiles[:, 0:1, :] - top[None]), axis=0)
    picked = jnp.sum(tiles[:, 2:3, :], axis=0)
    return top, total, picked


def as_tile(top, total, picked):
    row = lax.broadcasted_iota(jnp.int32, (8, 128), 0)
    return jnp.where(row == 0, top, jnp.where(row == 1, total, picked))


def kernel(
    hid, w_hbm, tgt, dh_out, dw_hbm, loss_out,
    w, tcol, gat, xs, xt, lp, rb, lown, sta, stz, mt, lt, es, eb, gb, ac, pf, tf, cs, cr, un, zs, za, zb, zsum, zq, zr, dw, pk,
    ss, rs, local,
):
    y = lax.axis_index("section")
    v = lax.axis_index("vocab")
    zl = lax.axis_index("rep")
    c = lax.rem(v, 2)
    zh = lax.rem(lax.div(v, 2), 4)
    x = lax.div(v, 8)
    z = zh * 4 + zl
    slot = zl * 4 + zh
    other = 1 - c

    def at(x=x, y=y, z=z, c=c):
        x, y, z = lax.rem(x + 4, 4), lax.rem(y + 4, 4), lax.rem(z + 16, 16)
        return (y, (x * 4 + lax.div(z, 4)) * 2 + c, lax.rem(z, 4))

    copies = []

    def send(src, dst, dest):
        k = len(copies)
        copy = pltpu.make_async_remote_copy(
            src, dst, ss.at[k], rs.at[k], device_id=dest, device_id_type=MESH
        )
        copy.start()
        copies.append(copy)
        return copy

    def mate(k):
        n = lax.rem(x * 2 + c + k, 8)
        return at(x=lax.div(n, 2), c=lax.rem(n, 2))

    partners = (
        [at(z=z + k) for k in FAR_FIRST]
        + [at(x=x + k, z=z + t) for k in (2, 1, 3) for t in (2, -2, 1, -1)]
        + [mate(k) for k in range(1, 8)]
        + [at(y=y + k) for k in (2, 1, 3)]
    )
    barrier = pltpu.get_barrier_semaphore()
    for p in partners:
        pl.semaphore_signal(barrier, inc=1, device_id=p, device_id_type=MESH)
    w_copy = pltpu.make_async_copy(w_hbm, w, local.at[0])
    w_copy.start()
    h = hid[...].astype(F32)
    for i in range(3):
        for j in range(16):
            pk[j : j + 1, i * 128 : (i + 1) * 128] = h[i : i + 1, j * 128 : (j + 1) * 128]
    gat[x, slot] = pk[...].astype(BF16)
    pl.semaphore_wait(barrier, len(partners))

    own_block = gat.at[x, slot]
    first = [send(own_block, own_block, at(z=z + 4 * k)) for k in (2, 1, 3)]

    @pl.loop(0, 96)
    def _(n):
        xx, cc, i, ll = n // 24, (n // 12) % 2, (n // 4) % 3, n % 4
        token = 3 * (xx * 32 + cc * 4 + ll) + i
        for hh in range(4):
            tcol[xx, pl.ds((n % 24) * 4 + hh, 1), :] = jnp.full((1, 128), tgt[token + 24 * hh])

    first_col = (v * 4 + zl) * 512

    def is_target(column):
        return lax.broadcasted_iota(jnp.int32, (96, 512), 1) + first_col == column

    def by_weight(rows):
        part = lax.dot_general(rows, w[...], (((1,), (1,)), ((), ())), preferred_element_type=F32)
        return part.reshape(2, 48, 2048)

    w_copy.wait()

    @pl.loop(0, 4)
    def _(k):
        tf[k] = by_weight(is_target(tcol[k][:, 0:1]).astype(F32).astype(BF16))

    for t in first:
        t.wait_recv()

    own_set = gat.at[x, pl.ds(zl * 4, 4)]
    low, high = gat.at[x, pl.ds(zl * 4, 2)], gat.at[x, pl.ds(zl * 4 + 2, 2)]
    arrivals = {}
    for k in (0, 1, 3, 2):
        arrivals[k] = [send(own_set, own_set, at(x=x + k))] if k else []
        arrivals[k] += [
            send(low, low, at(x=x + k, z=z + 2)),
            send(high, high, at(x=x + k, z=z - 2)),
            send(own_set, own_set, at(x=x + k, z=z + 1)),
            send(own_set, own_set, at(x=x + k, z=z - 1)),
        ]
    swap = swap_matrix()
    sib = {}

    def slab_from(k):
        return lax.rem(x - k + 4, 4)

    def unpack(k):
        for t in arrivals[k]:
            t.wait_recv()
        n = slab_from(k)
        turned = jnp.dot(swap, gat[n].reshape(256, 384), preferred_element_type=F32).astype(BF16)
        for i in range(3):
            for j in range(16):
                xs[n * 2 + c, i * 16 : (i + 1) * 16, j * 128 : (j + 1) * 128] = turned[
                    j * 16 : (j + 1) * 16, i * 128 : (i + 1) * 128
                ]
        group = xs.at[n * 2 + c]
        sib[k] = send(group, group, at(c=other))

    over_y = {}

    def slab_logits(k):
        sib[k].wait_recv()
        n = slab_from(k)
        lp[n] = jnp.dot(xs[pl.ds(n * 2, 2)].reshape(96, 2048), w[...], preferred_element_type=F32)
        over_y[k] = [
            send(lp.at[n, pl.ds(lax.rem(y + t, 4) * 24, 24)], rb.at[t - 1, n], at(y=y + t)) for t in (2, 1, 3)
        ]

    unpack(0)
    slab_logits(0)
    unpack(1)
    unpack(3)
    slab_logits(1)
    slab_logits(3)
    unpack(2)
    slab_logits(2)
    for k in (0, 1, 3, 2):
        for t in over_y[k]:
            t.wait_recv()
        n = slab_from(k)
        own = lp[n, pl.ds(pl.multiple_of(y * 24, 8), 24), :]
        lown[n] = (own + rb[0, n]) + (rb[1, n] + rb[2, n])

    logits = lown[...].reshape(96, 512)
    targets = tcol[:, pl.ds(pl.multiple_of(y * 24, 8), 24), :].reshape(96, 128)[:, 0:1]
    own_top = jnp.max(logits, axis=1, keepdims=True)
    powers = jnp.exp(logits - own_top)
    own_total = jnp.sum(powers, axis=1, keepdims=True)
    own_pick = jnp.sum(jnp.where(is_target(targets), logits, 0.0), axis=1, keepdims=True)
    lane = lax.broadcasted_iota(jnp.int32, (96, 128), 1)
    cols = jnp.where(lane == 0, own_top, jnp.where(lane == 1, own_total, own_pick))
    cols = jnp.concatenate([cols, jnp.ones((32, 128), F32)], axis=0)
    tile = cols.T[:8]
    sta[x * 2 + c] = tile
    mates = [send(sta.at[x * 2 + c], sta.at[x * 2 + c], mate(k)) for k in range(1, 8)]
    es[y] = powers.astype(BF16)
    mt[y] = tile
    over_y = [send(es.at[y], es.at[y], at(y=y + t)) for t in (2, 1, 3)]
    tops = [send(mt.at[y], mt.at[y], at(y=y + t)) for t in (2, 1, 3)]
    for t in mates:
        t.wait_recv()
    stz[z] = as_tile(*merge(sta[...]))
    over_z = [send(stz.at[z], stz.at[z], at(z=z + k)) for k in FAR_FIRST]

    for t in over_y:
        t.wait_recv()
    shares = [es[s].astype(F32) for s in range(4)]
    for k in range(4):
        eb[k] = jnp.concatenate([g[k * 24 : (k + 1) * 24] for g in shares], axis=0).astype(BF16)

    @pl.loop(0, 4)
    def _(k):
        pf[k] = by_weight(eb[k])

    for t in over_z:
        t.wait_recv()
    top, total, picked = merge(stz[...])
    lt[y] = as_tile(top + jnp.log(total), picked, picked)
    totals = [send(lt.at[y], lt.at[y], at(y=y + t)) for t in (2, 1, 3)]

    @pl.loop(0, 8)
    def _(n):
        cut = pl.ds(pl.multiple_of(n * 256, 256), 256)
        xt[n] = xs[:, :, cut].reshape(384, 256).T

    for t in tops + totals:
        t.wait_recv()
    for s in range(4):
        log_total = lt[s, 0:1, :]
        factor = jnp.exp(mt[s, 0:1, :] - log_total) * (1.0 + 2.0 * Z_WEIGHT * log_total)
        turned = jnp.broadcast_to(factor, (128, 128)).T
        for k in range(4):
            ac[k, s * 24 : (s + 1) * 24, :] = turned[k * 24 : (k + 1) * 24]

    def scaled(n, half):
        factor = ac[n, pl.ds(pl.multiple_of(half * 48, 8), 48), :][:, 0:1]
        return pf[n, half] * factor - tf[n, half]

    ks = (2, 1, 3, 0)
    over_c = []
    for d, k in enumerate(ks):
        cs[d] = scaled(lax.rem(x + k, 4), other).astype(BF16)
        over_c.append(send(cs.at[d], cr.at[d], at(c=other)))
    next_set, last_set, far = lax.rem(zl + 1, 4) * 4, lax.rem(zl + 3, 4) * 4, lax.rem(zl + 2, 4) * 4
    moves = []
    for d, k in enumerate(ks):
        over_c[d].wait_recv()
        part = (scaled(lax.rem(x + k, 4), c) + cr[d].astype(F32)).astype(BF16)
        for i in range(3):
            for j in range(16):
                un[j * 16 : (j + 1) * 16, i * 128 : (i + 1) * 128] = part[
                    i * 16 : (i + 1) * 16, j * 128 : (j + 1) * 128
                ]
        zs[d] = jnp.dot(swap, un[...], preferred_element_type=F32).astype(BF16).reshape(16, 16, 384)
        if k:
            moves.append(send(zs.at[d, pl.ds(zl * 4, 4)], za.at[k, 0], at(x=x + k)))
        moves += [
            send(zs.at[d, pl.ds(far, 2)], zb.at[k, 0], at(x=x + k, z=z - 2)),
            send(zs.at[d, pl.ds(far + 2, 2)], zb.at[k, 1], at(x=x + k, z=z + 2)),
            send(zs.at[d, pl.ds(next_set, 4)], za.at[k, 1], at(x=x + k, z=z + 1)),
            send(zs.at[d, pl.ds(last_set, 4)], za.at[k, 2], at(x=x + k, z=z - 1)),
        ]

    for k in range(4):
        grads = eb[k].astype(F32) * ac[k][:, 0:1] - is_target(tcol[k][:, 0:1]).astype(F32)
        gb[k] = grads.astype(BF16)

    @pl.loop(0, 8)
    def _(n):
        cut = pl.ds(pl.multiple_of(n * 256, 256), 256)
        dw[cut, :] = jnp.dot(xt[n], gb[...].reshape(384, 512), preferred_element_type=F32).astype(BF16)

    dw_copy = pltpu.make_async_copy(dw, dw_hbm, local.at[1])
    dw_copy.start()

    lane = lax.broadcasted_iota(jnp.int32, (1, 128), 1)
    row_loss = jnp.zeros((1, 128), F32)
    for s in range(4):
        log_total = lt[s, 0:1, :]
        row_loss = row_loss + (log_total - lt[s, 1:2, :] + Z_WEIGHT * log_total * log_total)
    loss_out[0] = jnp.sum(jnp.where(lane < 48, row_loss, 0.0)) / MB_TOK
    loss_out[1] = jnp.sum(jnp.where((lane >= 48) & (lane < 96), row_loss, 0.0)) / MB_TOK

    for t in moves:
        t.wait_recv()
    acc = zs[3, pl.ds(zl * 4, 4)].astype(F32)
    for k in range(4):
        for n in range(0 if k else 1, 3):
            acc = acc + za[k, n].astype(F32)
        acc = acc + zb[k].reshape(4, 16, 384).astype(F32)
    zsum[...] = acc
    zq[...] = acc.astype(BF16)

    moves = [send(zq.at[lax.rem(zh + k, 4)], zr.at[k - 1], at(z=z + 4 * k)) for k in (2, 1, 3)]
    for t in moves:
        t.wait_recv()
    pk[...] = zsum[zh] + zr[0].astype(F32) + zr[1].astype(F32) + zr[2].astype(F32)
    rows = []
    for i in range(3):
        rows.append(jnp.concatenate([pk[j : j + 1, i * 128 : (i + 1) * 128] for j in range(16)], axis=1))
    dh_out[...] = jnp.concatenate(rows, axis=0).astype(BF16)

    for t in copies:
        t.wait_send()
    dw_copy.wait()


FAR_FIRST = (8, 7, 9, 6, 10, 5, 11, 4, 12, 3, 13, 2, 14, 1, 15)
N_COPIES = 3 + 19 + 4 + 12 + 7 + 3 + 3 + 15 + 3 + 4 + 19 + 3


def on_device(hidden, head_weight, targets):
    vmem = pl.BlockSpec(memory_space=pltpu.VMEM)
    smem = pl.BlockSpec(memory_space=pltpu.SMEM)
    hbm = pl.BlockSpec(memory_space=pl.ANY)
    scratch = [
        ((2048, 512), BF16),
        ((4, 96, 128), jnp.int32),
        ((4, 16, 16, 384), BF16),
        ((8, 48, 2048), BF16),
        ((8, 256, 384), BF16),
        ((4, 96, 512), F32),
        ((3, 4, 24, 512), F32),
        ((4, 24, 512), F32),
        ((8, 8, 128), F32),
        ((16, 8, 128), F32),
        ((4, 8, 128), F32),
        ((4, 8, 128), F32),
        ((4, 96, 512), BF16),
        ((4, 96, 512), BF16),
        ((4, 96, 512), BF16),
        ((4, 96, 128), F32),
        ((4, 2, 48, 2048), F32),
        ((4, 2, 48, 2048), F32),
        ((4, 48, 2048), BF16),
        ((4, 48, 2048), BF16),
        ((256, 384), BF16),
        ((4, 16, 16, 384), BF16),
        ((4, 3, 4, 16, 384), BF16),
        ((4, 2, 2, 16, 384), BF16),
        ((4, 16, 384), F32),
        ((4, 16, 384), BF16),
        ((3, 16, 384), BF16),
        ((2048, 512), BF16),
        ((16, 384), F32),
    ]
    return pl.pallas_call(
        kernel,
        out_shape=(
            jax.ShapeDtypeStruct((3, 2048), BF16),
            jax.ShapeDtypeStruct((2048, 512), BF16),
            jax.ShapeDtypeStruct((2,), F32),
        ),
        in_specs=[vmem, hbm, smem],
        out_specs=(vmem, hbm, smem),
        scratch_shapes=[pltpu.VMEM(s, t) for s, t in scratch]
        + [pltpu.SemaphoreType.DMA((N_COPIES,)), pltpu.SemaphoreType.DMA((N_COPIES,)), pltpu.SemaphoreType.DMA((2,))],
        compiler_params=pltpu.CompilerParams(
            collective_id=0, has_side_effects=True, vmem_limit_bytes=58 * 1024 * 1024
        ),
        name="head",
    )(hidden, head_weight, targets)


def solution(mesh):
    return jax.shard_map(
        on_device,
        mesh=mesh,
        in_specs=(P(("vocab", "rep"), "section"), P("section", ("vocab", "rep")), P()),
        out_specs=(P(("vocab", "rep"), "section"), P("section", ("vocab", "rep")), P()),
        check_vma=False,
    )
```

```python
import jax
import jax.numpy as jnp
from jax import lax
from jax.experimental import pallas as pl
from jax.experimental.pallas import tpu as pltpu
from jax.sharding import PartitionSpec as P

MESH = pl.DeviceIdType.MESH
F32, BF16 = jnp.float32, jnp.bfloat16
Z_WEIGHT = 0.01
MB_TOK = 192


def swap_matrix():
    row = lax.broadcasted_iota(jnp.int32, (256, 256), 0)
    col = lax.broadcasted_iota(jnp.int32, (256, 256), 1)
    return jnp.where(col == (row % 16) * 16 + row // 16, 1.0, 0.0).astype(BF16)


def merge(tiles):
    top = jnp.max(tiles[:, 0:1, :], axis=0)
    total = jnp.sum(tiles[:, 1:2, :] * jnp.exp(tiles[:, 0:1, :] - top[None]), axis=0)
    picked = jnp.sum(tiles[:, 2:3, :], axis=0)
    return top, total, picked


def as_tile(top, total, picked):
    row = lax.broadcasted_iota(jnp.int32, (8, 128), 0)
    return jnp.where(row == 0, top, jnp.where(row == 1, total, picked))


def kernel(
    hid, w_hbm, tgt, dh_out, dw_hbm, loss_out,
    w, tcol, gat, xs, xt, lp, rb, lown, sta, stz, mt, lt, es, eb, gb, ac, pf, tf, cs, cr, un, zs, za, zb, zsum, zq, zr, dw, pk,
    ss, rs, local,
):
    y = lax.axis_index("section")
    v = lax.axis_index("vocab")
    zl = lax.axis_index("rep")
    c = lax.rem(v, 2)
    zh = lax.rem(lax.div(v, 2), 4)
    x = lax.div(v, 8)
    z = zh * 4 + zl
    slot = zl * 4 + zh
    other = 1 - c

    def at(x=x, y=y, z=z, c=c):
        x, y, z = lax.rem(x + 4, 4), lax.rem(y + 4, 4), lax.rem(z + 16, 16)
        return (y, (x * 4 + lax.div(z, 4)) * 2 + c, lax.rem(z, 4))

    copies = []
    sent = []

    def wait_sends():
        while len(sent) < len(copies):
            copies[len(sent)].wait_send()
            sent.append(True)

    def send(src, dst, dest):
        k = len(copies)
        copy = pltpu.make_async_remote_copy(
            src, dst, ss.at[k], rs.at[k], device_id=dest, device_id_type=MESH
        )
        copy.start()
        copies.append(copy)
        return copy

    def mate(k):
        n = lax.rem(x * 2 + c + k, 8)
        return at(x=lax.div(n, 2), c=lax.rem(n, 2))

    partners = (
        [at(z=z + k) for k in FAR_FIRST]
        + [at(x=x + k, z=z + t) for k in (2, 1, 3) for t in (2, -2, 1, -1)]
        + [mate(k) for k in range(1, 8)]
        + [at(y=y + k) for k in (2, 1, 3)]
    )
    barrier = pltpu.get_barrier_semaphore()
    for p in partners:
        pl.semaphore_signal(barrier, inc=1, device_id=p, device_id_type=MESH)
    w_copy = pltpu.make_async_copy(w_hbm, w, local.at[0])
    w_copy.start()
    h = hid[...].astype(F32)
    for i in range(3):
        for j in range(16):
            pk[j : j + 1, i * 128 : (i + 1) * 128] = h[i : i + 1, j * 128 : (j + 1) * 128]
    gat[x, slot] = pk[...].astype(BF16)
    pl.semaphore_wait(barrier, len(partners))

    own_block = gat.at[x, slot]
    first = [send(own_block, own_block, at(z=z + 4 * k)) for k in (2, 1, 3)]

    @pl.loop(0, 96)
    def _(n):
        xx, cc, i, ll = n // 24, (n // 12) % 2, (n // 4) % 3, n % 4
        token = 3 * (xx * 32 + cc * 4 + ll) + i
        for hh in range(4):
            tcol[xx, pl.ds((n % 24) * 4 + hh, 1), :] = jnp.full((1, 128), tgt[token + 24 * hh])

    first_col = (v * 4 + zl) * 512

    def is_target(column):
        return lax.broadcasted_iota(jnp.int32, (96, 512), 1) + first_col == column

    def by_weight(rows):
        part = lax.dot_general(rows, w[...], (((1,), (1,)), ((), ())), preferred_element_type=F32)
        return part.reshape(2, 48, 2048)

    w_copy.wait()

    @pl.loop(0, 4)
    def _(k):
        tf[k] = by_weight(is_target(tcol[k][:, 0:1]).astype(F32).astype(BF16))

    for t in first:
        t.wait_recv()

    own_set = gat.at[x, pl.ds(zl * 4, 4)]
    low, high = gat.at[x, pl.ds(zl * 4, 2)], gat.at[x, pl.ds(zl * 4 + 2, 2)]
    arrivals = {}

    def send_set(k):
        arrivals[k] = [send(own_set, own_set, at(x=x + k))] if k else []
        arrivals[k] += [
            send(low, low, at(x=x + k, z=z + 2)),
            send(high, high, at(x=x + k, z=z - 2)),
            send(own_set, own_set, at(x=x + k, z=z + 1)),
            send(own_set, own_set, at(x=x + k, z=z - 1)),
        ]

    send_set(0)
    send_set(1)
    send_set(3)
    send_set(2)
    swap = swap_matrix()
    sib = {}

    def slab_from(k):
        return lax.rem(x - k + 4, 4)

    def unpack(k):
        for t in arrivals[k]:
            t.wait_recv()
        n = slab_from(k)
        turned = jnp.dot(swap, gat[n].reshape(256, 384), preferred_element_type=F32).astype(BF16)
        for i in range(3):
            for j in range(16):
                xs[n * 2 + c, i * 16 : (i + 1) * 16, j * 128 : (j + 1) * 128] = turned[
                    j * 16 : (j + 1) * 16, i * 128 : (i + 1) * 128
                ]
        group = xs.at[n * 2 + c]
        sib[k] = send(group, group, at(c=other))

    over_y = {}

    def slab_logits(k):
        sib[k].wait_recv()
        n = slab_from(k)
        lp[n] = jnp.dot(xs[pl.ds(n * 2, 2)].reshape(96, 2048), w[...], preferred_element_type=F32)
        over_y[k] = [
            send(lp.at[n, pl.ds(lax.rem(y + t, 4) * 24, 24)], rb.at[t - 1, n], at(y=y + t)) for t in (2, 1, 3)
        ]

    unpack(0)
    slab_logits(0)
    unpack(1)
    unpack(3)
    slab_logits(1)
    slab_logits(3)
    unpack(2)
    slab_logits(2)
    for k in (0, 1, 3, 2):
        for t in over_y[k]:
            t.wait_recv()
        n = slab_from(k)
        own = lp[n, pl.ds(pl.multiple_of(y * 24, 8), 24), :]
        lown[n] = (own + rb[0, n]) + (rb[1, n] + rb[2, n])

    logits = lown[...].reshape(96, 512)
    targets = tcol[:, pl.ds(pl.multiple_of(y * 24, 8), 24), :].reshape(96, 128)[:, 0:1]
    own_top = jnp.max(logits, axis=1, keepdims=True)
    powers = jnp.exp(logits - own_top)
    own_total = jnp.sum(powers, axis=1, keepdims=True)
    own_pick = jnp.sum(jnp.where(is_target(targets), logits, 0.0), axis=1, keepdims=True)
    lane = lax.broadcasted_iota(jnp.int32, (96, 128), 1)
    cols = jnp.where(lane == 0, own_top, jnp.where(lane == 1, own_total, own_pick))
    cols = jnp.concatenate([cols, jnp.ones((32, 128), F32)], axis=0)
    tile = cols.T[:8]
    sta[x * 2 + c] = tile
    mates = [send(sta.at[x * 2 + c], sta.at[x * 2 + c], mate(k)) for k in range(1, 8)]
    es[y] = powers.astype(BF16)
    mt[y] = tile
    over_y = [send(es.at[y], es.at[y], at(y=y + t)) for t in (2, 1, 3)]
    tops = [send(mt.at[y], mt.at[y], at(y=y + t)) for t in (2, 1, 3)]
    for t in mates:
        t.wait_recv()
    stz[z] = as_tile(*merge(sta[...]))
    over_z = [send(stz.at[z], stz.at[z], at(z=z + k)) for k in FAR_FIRST]

    for t in over_y:
        t.wait_recv()
    shares = [es[s].astype(F32) for s in range(4)]
    for k in range(4):
        eb[k] = jnp.concatenate([g[k * 24 : (k + 1) * 24] for g in shares], axis=0).astype(BF16)

    @pl.loop(0, 4)
    def _(k):
        pf[k] = by_weight(eb[k])

    for t in over_z:
        t.wait_recv()
    top, total, picked = merge(stz[...])
    lt[y] = as_tile(top + jnp.log(total), picked, picked)
    totals = [send(lt.at[y], lt.at[y], at(y=y + t)) for t in (2, 1, 3)]

    @pl.loop(0, 8)
    def _(n):
        cut = pl.ds(pl.multiple_of(n * 256, 256), 256)
        xt[n] = xs[:, :, cut].reshape(384, 256).T

    for t in tops + totals:
        t.wait_recv()
    for s in range(4):
        log_total = lt[s, 0:1, :]
        factor = jnp.exp(mt[s, 0:1, :] - log_total) * (1.0 + 2.0 * Z_WEIGHT * log_total)
        turned = jnp.broadcast_to(factor, (128, 128)).T
        for k in range(4):
            ac[k, s * 24 : (s + 1) * 24, :] = turned[k * 24 : (k + 1) * 24]

    def scaled(n, half):
        factor = ac[n, pl.ds(pl.multiple_of(half * 48, 8), 48), :][:, 0:1]
        return pf[n, half] * factor - tf[n, half]

    ks = (2, 1, 3, 0)
    over_c = []
    for d, k in enumerate(ks):
        cs[d] = scaled(lax.rem(x + k, 4), other).astype(BF16)
        over_c.append(send(cs.at[d], cr.at[d], at(c=other)))
    next_set, last_set, far = lax.rem(zl + 1, 4) * 4, lax.rem(zl + 3, 4) * 4, lax.rem(zl + 2, 4) * 4
    moves = []
    for d, k in enumerate(ks):
        over_c[d].wait_recv()
        part = (scaled(lax.rem(x + k, 4), c) + cr[d].astype(F32)).astype(BF16)
        for i in range(3):
            for j in range(16):
                un[j * 16 : (j + 1) * 16, i * 128 : (i + 1) * 128] = part[
                    i * 16 : (i + 1) * 16, j * 128 : (j + 1) * 128
                ]
        zs[d] = jnp.dot(swap, un[...], preferred_element_type=F32).astype(BF16).reshape(16, 16, 384)
        if k:
            moves.append(send(zs.at[d, pl.ds(zl * 4, 4)], za.at[k, 0], at(x=x + k)))
        moves += [
            send(zs.at[d, pl.ds(far, 2)], zb.at[k, 0], at(x=x + k, z=z - 2)),
            send(zs.at[d, pl.ds(far + 2, 2)], zb.at[k, 1], at(x=x + k, z=z + 2)),
            send(zs.at[d, pl.ds(next_set, 4)], za.at[k, 1], at(x=x + k, z=z + 1)),
            send(zs.at[d, pl.ds(last_set, 4)], za.at[k, 2], at(x=x + k, z=z - 1)),
        ]

    for k in range(4):
        grads = eb[k].astype(F32) * ac[k][:, 0:1] - is_target(tcol[k][:, 0:1]).astype(F32)
        gb[k] = grads.astype(BF16)

    @pl.loop(0, 8)
    def _(n):
        cut = pl.ds(pl.multiple_of(n * 256, 256), 256)
        dw[cut, :] = jnp.dot(xt[n], gb[...].reshape(384, 512), preferred_element_type=F32).astype(BF16)

    dw_copy = pltpu.make_async_copy(dw, dw_hbm, local.at[1])
    dw_copy.start()

    lane = lax.broadcasted_iota(jnp.int32, (1, 128), 1)
    row_loss = jnp.zeros((1, 128), F32)
    for s in range(4):
        log_total = lt[s, 0:1, :]
        row_loss = row_loss + (log_total - lt[s, 1:2, :] + Z_WEIGHT * log_total * log_total)
    loss_out[0] = jnp.sum(jnp.where(lane < 48, row_loss, 0.0)) / MB_TOK
    loss_out[1] = jnp.sum(jnp.where((lane >= 48) & (lane < 96), row_loss, 0.0)) / MB_TOK

    for t in moves:
        t.wait_recv()
    acc = zs[3, pl.ds(zl * 4, 4)].astype(F32)
    for k in range(4):
        for n in range(0 if k else 1, 3):
            acc = acc + za[k, n].astype(F32)
        acc = acc + zb[k].reshape(4, 16, 384).astype(F32)
    zsum[...] = acc
    zq[...] = acc.astype(BF16)

    moves = [send(zq.at[lax.rem(zh + k, 4)], zr.at[k - 1], at(z=z + 4 * k)) for k in (2, 1, 3)]
    dw_copy.wait()
    wait_sends()
    for t in moves:
        t.wait_recv()
    pk[...] = zsum[zh] + zr[0].astype(F32) + zr[1].astype(F32) + zr[2].astype(F32)
    rows = []
    for i in range(3):
        rows.append(jnp.concatenate([pk[j : j + 1, i * 128 : (i + 1) * 128] for j in range(16)], axis=1))
    dh_out[...] = jnp.concatenate(rows, axis=0).astype(BF16)

    wait_sends()


FAR_FIRST = (8, 7, 9, 6, 10, 5, 11, 4, 12, 3, 13, 2, 14, 1, 15)
N_COPIES = 3 + 19 + 4 + 12 + 7 + 3 + 3 + 15 + 3 + 4 + 19 + 3


def on_device(hidden, head_weight, targets):
    vmem = pl.BlockSpec(memory_space=pltpu.VMEM)
    smem = pl.BlockSpec(memory_space=pltpu.SMEM)
    hbm = pl.BlockSpec(memory_space=pltpu.HBM)
    anywhere = pl.BlockSpec(memory_space=pl.ANY)
    scratch = [
        ((2048, 512), BF16),
        ((4, 96, 128), jnp.int32),
        ((4, 16, 16, 384), BF16),
        ((8, 48, 2048), BF16),
        ((8, 256, 384), BF16),
        ((4, 96, 512), F32),
        ((3, 4, 24, 512), F32),
        ((4, 24, 512), F32),
        ((8, 8, 128), F32),
        ((16, 8, 128), F32),
        ((4, 8, 128), F32),
        ((4, 8, 128), F32),
        ((4, 96, 512), BF16),
        ((4, 96, 512), BF16),
        ((4, 96, 512), BF16),
        ((4, 96, 128), F32),
        ((4, 2, 48, 2048), F32),
        ((4, 2, 48, 2048), F32),
        ((4, 48, 2048), BF16),
        ((4, 48, 2048), BF16),
        ((256, 384), BF16),
        ((4, 16, 16, 384), BF16),
        ((4, 3, 4, 16, 384), BF16),
        ((4, 2, 2, 16, 384), BF16),
        ((4, 16, 384), F32),
        ((4, 16, 384), BF16),
        ((3, 16, 384), BF16),
        ((2048, 512), BF16),
        ((16, 384), F32),
    ]
    return pl.pallas_call(
        kernel,
        out_shape=(
            jax.ShapeDtypeStruct((3, 2048), BF16),
            jax.ShapeDtypeStruct((2048, 512), BF16),
            jax.ShapeDtypeStruct((2,), F32),
        ),
        in_specs=[vmem, hbm, smem],
        out_specs=(vmem, anywhere, smem),
        scratch_shapes=[pltpu.VMEM(s, t) for s, t in scratch]
        + [pltpu.SemaphoreType.DMA((N_COPIES,)), pltpu.SemaphoreType.DMA((N_COPIES,)), pltpu.SemaphoreType.DMA((2,))],
        compiler_params=pltpu.CompilerParams(
            collective_id=0, has_side_effects=True, vmem_limit_bytes=50 * 1024 * 1024
        ),
        name="head",
    )(hidden, head_weight, targets)


def solution(mesh):
    return jax.shard_map(
        on_device,
        mesh=mesh,
        in_specs=(P(("vocab", "rep"), "section"), P("section", ("vocab", "rep")), P()),
        out_specs=(P(("vocab", "rep"), "section"), P("section", ("vocab", "rep")), P()),
        check_vma=False,
    )
```

```python
import jax
import jax.numpy as jnp
from jax import lax
from jax.experimental import pallas as pl
from jax.experimental.pallas import tpu as pltpu
from jax.sharding import PartitionSpec as P

MESH = pl.DeviceIdType.MESH
F32, BF16 = jnp.float32, jnp.bfloat16
Z_WEIGHT = 0.01
MB_TOK = 192


def swap_matrix():
    row = lax.broadcasted_iota(jnp.int32, (256, 256), 0)
    col = lax.broadcasted_iota(jnp.int32, (256, 256), 1)
    return jnp.where(col == (row % 16) * 16 + row // 16, 1.0, 0.0).astype(BF16)


def merge(tiles):
    top = jnp.max(tiles[:, 0:1, :], axis=0)
    total = jnp.sum(tiles[:, 1:2, :] * jnp.exp(tiles[:, 0:1, :] - top[None]), axis=0)
    picked = jnp.sum(tiles[:, 2:3, :], axis=0)
    return top, total, picked


def as_tile(top, total, picked):
    row = lax.broadcasted_iota(jnp.int32, (8, 128), 0)
    return jnp.where(row == 0, top, jnp.where(row == 1, total, picked))


def kernel(
    hid, w_hbm, tgt, dh_out, dw_hbm, loss_out,
    w, tcol, gat, xs, xt, lp, rb, lown, sta, stz, mt, lt, es, eb, gb, ac, pf, tf, cs, cr, un, zs, za, zb, zsum, zq, zr, dw, pk, ct, rt, cb,
    ss, rs, local,
):
    y = lax.axis_index("section")
    v = lax.axis_index("vocab")
    zl = lax.axis_index("rep")
    c = lax.rem(v, 2)
    zh = lax.rem(lax.div(v, 2), 4)
    x = lax.div(v, 8)
    z = zh * 4 + zl
    slot = zl * 4 + zh
    other = 1 - c

    def at(x=x, y=y, z=z, c=c):
        x, y, z = lax.rem(x + 4, 4), lax.rem(y + 4, 4), lax.rem(z + 16, 16)
        return (y, (x * 4 + lax.div(z, 4)) * 2 + c, lax.rem(z, 4))

    copies = []
    sent = []

    def wait_sends():
        while len(sent) < len(copies):
            copies[len(sent)].wait_send()
            sent.append(True)

    def send(src, dst, dest):
        k = len(copies)
        copy = pltpu.make_async_remote_copy(
            src, dst, ss.at[k], rs.at[k], device_id=dest, device_id_type=MESH
        )
        copy.start()
        copies.append(copy)
        return copy

    def mate(k):
        n = lax.rem(x * 2 + c + k, 8)
        return at(x=lax.div(n, 2), c=lax.rem(n, 2))

    partners = (
        [at(z=z + k) for k in FAR_FIRST]
        + [at(x=x + k, z=z + t) for k in (2, 1, 3) for t in (2, -2, 1, -1)]
        + [mate(k) for k in range(1, 8)]
        + [at(y=y + k) for k in (2, 1, 3)]
    )
    barrier = pltpu.get_barrier_semaphore()
    for p in partners:
        pl.semaphore_signal(barrier, inc=1, device_id=p, device_id_type=MESH)
    w_copy = pltpu.make_async_copy(w_hbm, w, local.at[0])
    w_copy.start()
    h = hid[...].astype(F32)
    for i in range(3):
        for j in range(16):
            pk[j : j + 1, i * 128 : (i + 1) * 128] = h[i : i + 1, j * 128 : (j + 1) * 128]
    gat[x, slot] = pk[...].astype(BF16)
    pl.semaphore_wait(barrier, len(partners))

    own_block = gat.at[x, slot]
    first = [send(own_block, own_block, at(z=z + 4 * k)) for k in (2, 1, 3)]

    @pl.loop(0, 96)
    def _(n):
        xx, cc, i, ll = n // 24, (n // 12) % 2, (n // 4) % 3, n % 4
        token = 3 * (xx * 32 + cc * 4 + ll) + i
        for hh in range(4):
            tcol[xx, pl.ds((n % 24) * 4 + hh, 1), :] = jnp.full((1, 128), tgt[token + 24 * hh])

    first_col = (v * 4 + zl) * 512

    def is_target(column):
        return lax.broadcasted_iota(jnp.int32, (96, 512), 1) + first_col == column

    def by_weight(rows):
        part = lax.dot_general(rows, w[...], (((1,), (1,)), ((), ())), preferred_element_type=F32)
        return part.reshape(2, 48, 2048)

    w_copy.wait()

    target_parts = []
    for k in range(4):
        tf[k] = by_weight(is_target(tcol[k][:, 0:1]).astype(F32).astype(BF16))
        ct[k] = tf[k, other].astype(BF16)
        target_parts.append(send(ct.at[k], rt.at[k], at(c=other)))

    for t in first:
        t.wait_recv()

    own_set = gat.at[x, pl.ds(zl * 4, 4)]
    low, high = gat.at[x, pl.ds(zl * 4, 2)], gat.at[x, pl.ds(zl * 4 + 2, 2)]
    arrivals = {}

    def send_set(k):
        arrivals[k] = [send(own_set, own_set, at(x=x + k))] if k else []
        arrivals[k] += [
            send(low, low, at(x=x + k, z=z + 2)),
            send(high, high, at(x=x + k, z=z - 2)),
            send(own_set, own_set, at(x=x + k, z=z + 1)),
            send(own_set, own_set, at(x=x + k, z=z - 1)),
        ]

    send_set(0)
    send_set(1)
    send_set(3)
    send_set(2)
    swap = swap_matrix()
    sib = {}

    def slab_from(k):
        return lax.rem(x - k + 4, 4)

    def unpack(k):
        for t in arrivals[k]:
            t.wait_recv()
        n = slab_from(k)
        turned = jnp.dot(swap, gat[n].reshape(256, 384), preferred_element_type=F32).astype(BF16)
        for i in range(3):
            for j in range(16):
                xs[n * 2 + c, i * 16 : (i + 1) * 16, j * 128 : (j + 1) * 128] = turned[
                    j * 16 : (j + 1) * 16, i * 128 : (i + 1) * 128
                ]
        group = xs.at[n * 2 + c]
        sib[k] = send(group, group, at(c=other))

    over_y = {}

    def slab_logits(k):
        sib[k].wait_recv()
        n = slab_from(k)
        lp[n] = jnp.dot(xs[pl.ds(n * 2, 2)].reshape(96, 2048), w[...], preferred_element_type=F32)
        over_y[k] = [
            send(lp.at[n, pl.ds(lax.rem(y + t, 4) * 24, 24)], rb.at[t - 1, n], at(y=y + t)) for t in (2, 1, 3)
        ]

    unpack(0)
    slab_logits(0)
    unpack(1)
    unpack(3)
    slab_logits(1)
    slab_logits(3)
    unpack(2)
    slab_logits(2)
    for k in (0, 1, 3, 2):
        for t in over_y[k]:
            t.wait_recv()
        n = slab_from(k)
        own = lp[n, pl.ds(pl.multiple_of(y * 24, 8), 24), :]
        lown[n] = (own + rb[0, n]) + (rb[1, n] + rb[2, n])

    logits = lown[...].reshape(96, 512)
    targets = tcol[:, pl.ds(pl.multiple_of(y * 24, 8), 24), :].reshape(96, 128)[:, 0:1]
    own_top = jnp.max(logits, axis=1, keepdims=True)
    powers = jnp.exp(logits - own_top)
    own_total = jnp.sum(powers, axis=1, keepdims=True)
    own_pick = jnp.sum(jnp.where(is_target(targets), logits, 0.0), axis=1, keepdims=True)
    lane = lax.broadcasted_iota(jnp.int32, (96, 128), 1)
    cols = jnp.where(lane == 0, own_top, jnp.where(lane == 1, own_total, own_pick))
    cols = jnp.concatenate([cols, jnp.ones((32, 128), F32)], axis=0)
    tile = cols.T[:8]
    sta[x * 2 + c] = tile
    mates = [send(sta.at[x * 2 + c], sta.at[x * 2 + c], mate(k)) for k in range(1, 8)]
    cb[c] = tile
    pair = send(cb.at[c], cb.at[c], at(c=other))
    pair.wait_recv()
    chip_top = jnp.maximum(cb[0, 0:1, :], cb[1, 0:1, :])
    top_column = jnp.broadcast_to(chip_top, (128, 128)).T[:96, 0:1]
    es[y] = jnp.exp(logits - top_column).astype(BF16)
    mt[y] = jnp.broadcast_to(chip_top, (8, 128))
    over_y = [send(es.at[y], es.at[y], at(y=y + t)) for t in (2, 1, 3)]
    tops = [send(mt.at[y], mt.at[y], at(y=y + t)) for t in (2, 1, 3)]
    for t in mates:
        t.wait_recv()
    stz[z] = as_tile(*merge(sta[...]))
    over_z = [send(stz.at[z], stz.at[z], at(z=z + k)) for k in FAR_FIRST]

    @pl.loop(0, 8)
    def _(n):
        cut = pl.ds(pl.multiple_of(n * 256, 256), 256)
        xt[n] = xs[:, :, cut].reshape(384, 256).T

    for t in target_parts:
        t.wait_recv()

    @pl.loop(0, 4)
    def _(k):
        tf[k, c] = tf[k, c] + rt[k].astype(F32)

    for t in over_y:
        t.wait_recv()
    shares = [es[s].astype(F32) for s in range(4)]
    for k in range(4):
        eb[k] = jnp.concatenate([g[k * 24 : (k + 1) * 24] for g in shares], axis=0).astype(BF16)

    ks = (2, 1, 3, 0)
    over_c = []

    def partial_sums(d):
        n = lax.rem(x + ks[d], 4)
        pf[n] = by_weight(eb[n])
        cs[d] = pf[n, other].astype(BF16)
        over_c.append(send(cs.at[d], cr.at[d], at(c=other)))

    partial_sums(0)
    partial_sums(1)
    for t in over_z:
        t.wait_recv()
    top, total, picked = merge(stz[...])
    lt[y] = as_tile(top + jnp.log(total), picked, picked)
    totals = [send(lt.at[y], lt.at[y], at(y=y + t)) for t in (2, 1, 3)]

    partial_sums(2)
    partial_sums(3)
    for t in tops + totals:
        t.wait_recv()
    for s in range(4):
        log_total = lt[s, 0:1, :]
        factor = jnp.exp(mt[s, 0:1, :] - log_total) * (1.0 + 2.0 * Z_WEIGHT * log_total)
        turned = jnp.broadcast_to(factor, (128, 128)).T
        for k in range(4):
            ac[k, s * 24 : (s + 1) * 24, :] = turned[k * 24 : (k + 1) * 24]

    next_set, last_set, far = lax.rem(zl + 1, 4) * 4, lax.rem(zl + 3, 4) * 4, lax.rem(zl + 2, 4) * 4
    moves = []
    for d, k in enumerate(ks):
        over_c[d].wait_recv()
        n = lax.rem(x + k, 4)
        factor = ac[n, pl.ds(pl.multiple_of(c * 48, 8), 48), :][:, 0:1]
        part = ((pf[n, c] + cr[d].astype(F32)) * factor - tf[n, c]).astype(BF16)
        for i in range(3):
            for j in range(16):
                un[j * 16 : (j + 1) * 16, i * 128 : (i + 1) * 128] = part[
                    i * 16 : (i + 1) * 16, j * 128 : (j + 1) * 128
                ]
        zs[d] = jnp.dot(swap, un[...], preferred_element_type=F32).astype(BF16).reshape(16, 16, 384)
        if k:
            moves.append(send(zs.at[d, pl.ds(zl * 4, 4)], za.at[k, 0], at(x=x + k)))
        moves += [
            send(zs.at[d, pl.ds(far, 2)], zb.at[k, 0], at(x=x + k, z=z - 2)),
            send(zs.at[d, pl.ds(far + 2, 2)], zb.at[k, 1], at(x=x + k, z=z + 2)),
            send(zs.at[d, pl.ds(next_set, 4)], za.at[k, 1], at(x=x + k, z=z + 1)),
            send(zs.at[d, pl.ds(last_set, 4)], za.at[k, 2], at(x=x + k, z=z - 1)),
        ]

    for k in range(4):
        grads = eb[k].astype(F32) * ac[k][:, 0:1] - is_target(tcol[k][:, 0:1]).astype(F32)
        gb[k] = grads.astype(BF16)

    @pl.loop(0, 8)
    def _(n):
        cut = pl.ds(pl.multiple_of(n * 256, 256), 256)
        dw[cut, :] = jnp.dot(xt[n], gb[...].reshape(384, 512), preferred_element_type=F32).astype(BF16)

    dw_copy = pltpu.make_async_copy(dw, dw_hbm, local.at[1])
    dw_copy.start()

    lane = lax.broadcasted_iota(jnp.int32, (1, 128), 1)
    row_loss = jnp.zeros((1, 128), F32)
    for s in range(4):
        log_total = lt[s, 0:1, :]
        row_loss = row_loss + (log_total - lt[s, 1:2, :] + Z_WEIGHT * log_total * log_total)
    loss_out[0] = jnp.sum(jnp.where(lane < 48, row_loss, 0.0)) / MB_TOK
    loss_out[1] = jnp.sum(jnp.where((lane >= 48) & (lane < 96), row_loss, 0.0)) / MB_TOK

    for t in moves:
        t.wait_recv()
    acc = zs[3, pl.ds(zl * 4, 4)].astype(F32)
    for k in range(4):
        for n in range(0 if k else 1, 3):
            acc = acc + za[k, n].astype(F32)
        acc = acc + zb[k].reshape(4, 16, 384).astype(F32)
    zsum[...] = acc
    zq[...] = acc.astype(BF16)

    moves = [send(zq.at[lax.rem(zh + k, 4)], zr.at[k - 1], at(z=z + 4 * k)) for k in (2, 1, 3)]
    dw_copy.wait()
    wait_sends()
    for t in moves:
        t.wait_recv()
    pk[...] = zsum[zh] + zr[0].astype(F32) + zr[1].astype(F32) + zr[2].astype(F32)
    rows = []
    for i in range(3):
        rows.append(jnp.concatenate([pk[j : j + 1, i * 128 : (i + 1) * 128] for j in range(16)], axis=1))
    dh_out[...] = jnp.concatenate(rows, axis=0).astype(BF16)

    wait_sends()


FAR_FIRST = (8, 7, 9, 6, 10, 5, 11, 4, 12, 3, 13, 2, 14, 1, 15)
N_COPIES = 3 + 4 + 1 + 19 + 4 + 12 + 7 + 3 + 3 + 15 + 3 + 4 + 19 + 3


def on_device(hidden, head_weight, targets):
    vmem = pl.BlockSpec(memory_space=pltpu.VMEM)
    smem = pl.BlockSpec(memory_space=pltpu.SMEM)
    hbm = pl.BlockSpec(memory_space=pltpu.HBM)
    anywhere = pl.BlockSpec(memory_space=pl.ANY)
    scratch = [
        ((2048, 512), BF16),
        ((4, 96, 128), jnp.int32),
        ((4, 16, 16, 384), BF16),
        ((8, 48, 2048), BF16),
        ((8, 256, 384), BF16),
        ((4, 96, 512), F32),
        ((3, 4, 24, 512), F32),
        ((4, 24, 512), F32),
        ((8, 8, 128), F32),
        ((16, 8, 128), F32),
        ((4, 8, 128), F32),
        ((4, 8, 128), F32),
        ((4, 96, 512), BF16),
        ((4, 96, 512), BF16),
        ((4, 96, 512), BF16),
        ((4, 96, 128), F32),
        ((4, 2, 48, 2048), F32),
        ((4, 2, 48, 2048), F32),
        ((4, 48, 2048), BF16),
        ((4, 48, 2048), BF16),
        ((256, 384), BF16),
        ((4, 16, 16, 384), BF16),
        ((4, 3, 4, 16, 384), BF16),
        ((4, 2, 2, 16, 384), BF16),
        ((4, 16, 384), F32),
        ((4, 16, 384), BF16),
        ((3, 16, 384), BF16),
        ((2048, 512), BF16),
        ((16, 384), F32),
        ((4, 48, 2048), BF16),
        ((4, 48, 2048), BF16),
        ((2, 8, 128), F32),
    ]
    return pl.pallas_call(
        kernel,
        out_shape=(
            jax.ShapeDtypeStruct((3, 2048), BF16),
            jax.ShapeDtypeStruct((2048, 512), BF16),
            jax.ShapeDtypeStruct((2,), F32),
        ),
        in_specs=[vmem, hbm, smem],
        out_specs=(vmem, anywhere, smem),
        scratch_shapes=[pltpu.VMEM(s, t) for s, t in scratch]
        + [pltpu.SemaphoreType.DMA((N_COPIES,)), pltpu.SemaphoreType.DMA((N_COPIES,)), pltpu.SemaphoreType.DMA((2,))],
        compiler_params=pltpu.CompilerParams(
            collective_id=0, has_side_effects=True, vmem_limit_bytes=50 * 1024 * 1024
        ),
        name="head",
    )(hidden, head_weight, targets)


def solution(mesh):
    return jax.shard_map(
        on_device,
        mesh=mesh,
        in_specs=(P(("vocab", "rep"), "section"), P("section", ("vocab", "rep")), P()),
        out_specs=(P(("vocab", "rep"), "section"), P("section", ("vocab", "rep")), P()),
        check_vma=False,
    )
```

```python
import jax
import jax.numpy as jnp
from jax import lax
from jax.experimental import pallas as pl
from jax.experimental.pallas import tpu as pltpu
from jax.sharding import PartitionSpec as P

MESH = pl.DeviceIdType.MESH
F32, BF16 = jnp.float32, jnp.bfloat16
Z_WEIGHT = 0.01
MB_TOK = 192


def swap_matrix():
    row = lax.broadcasted_iota(jnp.int32, (256, 256), 0)
    col = lax.broadcasted_iota(jnp.int32, (256, 256), 1)
    return jnp.where(col == (row % 16) * 16 + row // 16, 1.0, 0.0).astype(BF16)


def merge(tiles):
    top = jnp.max(tiles[:, 0:1, :], axis=0)
    total = jnp.sum(tiles[:, 1:2, :] * jnp.exp(tiles[:, 0:1, :] - top[None]), axis=0)
    picked = jnp.sum(tiles[:, 2:3, :], axis=0)
    return top, total, picked


def as_tile(top, total, picked):
    row = lax.broadcasted_iota(jnp.int32, (8, 128), 0)
    return jnp.where(row == 0, top, jnp.where(row == 1, total, picked))


def kernel(
    hid, w_hbm, tgt, dh_out, dw_hbm, loss_out,
    w, tcol, gat, xs, xt, lp, rb, lown, sta, stz, mt, lt, es, eb, gb, ac, pf, tf, cs, cr, un, zs, za, zb, zsum, zq, zr, dw, pk, ct, rt, cb,
    ss, rs, local,
):
    y = lax.axis_index("section")
    v = lax.axis_index("vocab")
    zl = lax.axis_index("rep")
    c = lax.rem(v, 2)
    zh = lax.rem(lax.div(v, 2), 4)
    x = lax.div(v, 8)
    z = zh * 4 + zl
    slot = zl * 4 + zh
    other = 1 - c

    def at(x=x, y=y, z=z, c=c):
        x, y, z = lax.rem(x + 4, 4), lax.rem(y + 4, 4), lax.rem(z + 16, 16)
        return (y, (x * 4 + lax.div(z, 4)) * 2 + c, lax.rem(z, 4))

    copies = []
    sent = []

    def wait_sends():
        while len(sent) < len(copies):
            copies[len(sent)].wait_send()
            sent.append(True)

    def send(src, dst, dest):
        k = len(copies)
        copy = pltpu.make_async_remote_copy(
            src, dst, ss.at[k], rs.at[k], device_id=dest, device_id_type=MESH
        )
        copy.start()
        copies.append(copy)
        return copy

    def mate(k):
        n = lax.rem(x * 2 + c + k, 8)
        return at(x=lax.div(n, 2), c=lax.rem(n, 2))

    partners = (
        [at(z=z + k) for k in FAR_FIRST]
        + [at(x=x + k, z=z + t) for k in (2, 1, 3) for t in (2, -2, 1, -1)]
        + [mate(k) for k in range(1, 8)]
        + [at(y=y + k) for k in (2, 1, 3)]
    )
    barrier = pltpu.get_barrier_semaphore()
    for p in partners:
        pl.semaphore_signal(barrier, inc=1, device_id=p, device_id_type=MESH)
    w_copy = pltpu.make_async_copy(w_hbm, w, local.at[0])
    w_copy.start()
    h = hid[...].astype(F32)
    for i in range(3):
        for j in range(16):
            pk[j : j + 1, i * 128 : (i + 1) * 128] = h[i : i + 1, j * 128 : (j + 1) * 128]
    gat[x, slot] = pk[...].astype(BF16)
    pl.semaphore_wait(barrier, len(partners))

    own_block = gat.at[x, slot]
    first = [send(own_block, own_block, at(z=z + 4 * k)) for k in (2, 1, 3)]

    @pl.loop(0, 96)
    def _(n):
        xx, cc, i, ll = n // 24, (n // 12) % 2, (n // 4) % 3, n % 4
        token = 3 * (xx * 32 + cc * 4 + ll) + i
        for hh in range(4):
            tcol[xx, pl.ds((n % 24) * 4 + hh, 1), :] = jnp.full((1, 128), tgt[token + 24 * hh])

    first_col = (v * 4 + zl) * 512

    def is_target(column):
        return lax.broadcasted_iota(jnp.int32, (96, 512), 1) + first_col == column

    def by_weight(rows):
        part = lax.dot_general(rows, w[...], (((1,), (1,)), ((), ())), preferred_element_type=F32)
        return part.reshape(2, 48, 2048)

    w_copy.wait()

    target_parts = []
    for k in range(4):
        tf[k] = by_weight(is_target(tcol[k][:, 0:1]).astype(F32).astype(BF16))
        ct[k] = tf[k, other].astype(BF16)
        target_parts.append(send(ct.at[k], rt.at[k], at(c=other)))

    for t in first:
        t.wait_recv()

    own_set = gat.at[x, pl.ds(zl * 4, 4)]
    low, high = gat.at[x, pl.ds(zl * 4, 2)], gat.at[x, pl.ds(zl * 4 + 2, 2)]
    arrivals = {}

    def send_set(k):
        arrivals[k] = [send(own_set, own_set, at(x=x + k))] if k else []
        arrivals[k] += [
            send(low, low, at(x=x + k, z=z + 2)),
            send(high, high, at(x=x + k, z=z - 2)),
            send(own_set, own_set, at(x=x + k, z=z + 1)),
            send(own_set, own_set, at(x=x + k, z=z - 1)),
        ]

    send_set(0)
    send_set(1)
    send_set(3)
    send_set(2)
    swap = swap_matrix()
    sib = {}

    def slab_from(k):
        return lax.rem(x - k + 4, 4)

    def unpack(k):
        for t in arrivals[k]:
            t.wait_recv()
        n = slab_from(k)
        turned = jnp.dot(swap, gat[n].reshape(256, 384), preferred_element_type=F32).astype(BF16)
        for i in range(3):
            for j in range(16):
                xs[n * 2 + c, i * 16 : (i + 1) * 16, j * 128 : (j + 1) * 128] = turned[
                    j * 16 : (j + 1) * 16, i * 128 : (i + 1) * 128
                ]
        group = xs.at[n * 2 + c]
        sib[k] = send(group, group, at(c=other))

    over_y = {}

    def slab_logits(*ks):
        rows = []
        for k in ks:
            sib[k].wait_recv()
            rows.append(xs[pl.ds(slab_from(k) * 2, 2)].reshape(96, 2048))
        part = jnp.dot(jnp.concatenate(rows, axis=0), w[...], preferred_element_type=F32)
        for i, k in enumerate(ks):
            n = slab_from(k)
            lp[n] = part[i * 96 : (i + 1) * 96]
            over_y[k] = [
                send(lp.at[n, pl.ds(lax.rem(y + t, 4) * 24, 24)], rb.at[t - 1, n], at(y=y + t)) for t in (2, 1, 3)
            ]

    unpack(0)
    slab_logits(0)
    unpack(1)
    unpack(3)
    slab_logits(1, 3)
    unpack(2)
    slab_logits(2)
    for k in (0, 1, 3, 2):
        for t in over_y[k]:
            t.wait_recv()
        n = slab_from(k)
        own = lp[n, pl.ds(pl.multiple_of(y * 24, 8), 24), :]
        lown[n] = (own + rb[0, n]) + (rb[1, n] + rb[2, n])

    logits = lown[...].reshape(96, 512)
    targets = tcol[:, pl.ds(pl.multiple_of(y * 24, 8), 24), :].reshape(96, 128)[:, 0:1]
    own_top = jnp.max(logits, axis=1, keepdims=True)
    powers = jnp.exp(logits - own_top)
    own_total = jnp.sum(powers, axis=1, keepdims=True)
    own_pick = jnp.sum(jnp.where(is_target(targets), logits, 0.0), axis=1, keepdims=True)
    lane = lax.broadcasted_iota(jnp.int32, (96, 128), 1)
    cols = jnp.where(lane == 0, own_top, jnp.where(lane == 1, own_total, own_pick))
    cols = jnp.concatenate([cols, jnp.ones((32, 128), F32)], axis=0)
    tile = cols.T[:8]
    sta[x * 2 + c] = tile
    mates = [send(sta.at[x * 2 + c], sta.at[x * 2 + c], mate(k)) for k in range(1, 8)]
    cb[c] = tile
    pair = send(cb.at[c], cb.at[c], at(c=other))
    pair.wait_recv()
    chip_top = jnp.maximum(cb[0, 0:1, :], cb[1, 0:1, :])
    top_column = jnp.broadcast_to(chip_top, (128, 128)).T[:96, 0:1]
    es[y] = jnp.exp(logits - top_column).astype(BF16)
    mt[y] = jnp.broadcast_to(chip_top, (8, 128))
    over_y = [send(es.at[y], es.at[y], at(y=y + t)) for t in (2, 1, 3)]
    tops = [send(mt.at[y], mt.at[y], at(y=y + t)) for t in (2, 1, 3)]
    for t in mates:
        t.wait_recv()
    stz[z] = as_tile(*merge(sta[...]))
    over_z = [send(stz.at[z], stz.at[z], at(z=z + k)) for k in FAR_FIRST]

    @pl.loop(0, 8)
    def _(n):
        cut = pl.ds(pl.multiple_of(n * 256, 256), 256)
        xt[n] = xs[:, :, cut].reshape(384, 256).T

    for t in target_parts:
        t.wait_recv()

    @pl.loop(0, 4)
    def _(k):
        tf[k, c] = tf[k, c] + rt[k].astype(F32)

    for t in over_y:
        t.wait_recv()
    shares = [es[s].astype(F32) for s in range(4)]
    for k in range(4):
        eb[k] = jnp.concatenate([g[k * 24 : (k + 1) * 24] for g in shares], axis=0).astype(BF16)

    ks = (2, 1, 3, 0)
    over_c = []

    def partial_sums(d):
        n = lax.rem(x + ks[d], 4)
        pf[n] = by_weight(eb[n])
        cs[d] = pf[n, other].astype(BF16)
        over_c.append(send(cs.at[d], cr.at[d], at(c=other)))

    partial_sums(0)
    partial_sums(1)
    for t in over_z:
        t.wait_recv()
    top, total, picked = merge(stz[...])
    lt[y] = as_tile(top + jnp.log(total), picked, picked)
    totals = [send(lt.at[y], lt.at[y], at(y=y + t)) for t in (2, 1, 3)]

    partial_sums(2)
    partial_sums(3)
    for t in tops + totals:
        t.wait_recv()
    for s in range(4):
        log_total = lt[s, 0:1, :]
        factor = jnp.exp(mt[s, 0:1, :] - log_total) * (1.0 + 2.0 * Z_WEIGHT * log_total)
        turned = jnp.broadcast_to(factor, (128, 128)).T
        for k in range(4):
            ac[k, s * 24 : (s + 1) * 24, :] = turned[k * 24 : (k + 1) * 24]

    next_set, last_set, far = lax.rem(zl + 1, 4) * 4, lax.rem(zl + 3, 4) * 4, lax.rem(zl + 2, 4) * 4
    moves = []
    for d, k in enumerate(ks):
        over_c[d].wait_recv()
        n = lax.rem(x + k, 4)
        factor = ac[n, pl.ds(pl.multiple_of(c * 48, 8), 48), :][:, 0:1]
        part = ((pf[n, c] + cr[d].astype(F32)) * factor - tf[n, c]).astype(BF16)
        for i in range(3):
            for j in range(16):
                un[j * 16 : (j + 1) * 16, i * 128 : (i + 1) * 128] = part[
                    i * 16 : (i + 1) * 16, j * 128 : (j + 1) * 128
                ]
        zs[d] = jnp.dot(swap, un[...], preferred_element_type=F32).astype(BF16).reshape(16, 16, 384)
        if k:
            moves.append(send(zs.at[d, pl.ds(zl * 4, 4)], za.at[k, 0], at(x=x + k)))
        moves += [
            send(zs.at[d, pl.ds(far, 2)], zb.at[k, 0], at(x=x + k, z=z - 2)),
            send(zs.at[d, pl.ds(far + 2, 2)], zb.at[k, 1], at(x=x + k, z=z + 2)),
            send(zs.at[d, pl.ds(next_set, 4)], za.at[k, 1], at(x=x + k, z=z + 1)),
            send(zs.at[d, pl.ds(last_set, 4)], za.at[k, 2], at(x=x + k, z=z - 1)),
        ]

    for k in range(4):
        grads = eb[k].astype(F32) * ac[k][:, 0:1] - is_target(tcol[k][:, 0:1]).astype(F32)
        gb[k] = grads.astype(BF16)

    @pl.loop(0, 8)
    def _(n):
        cut = pl.ds(pl.multiple_of(n * 256, 256), 256)
        dw[cut, :] = jnp.dot(xt[n], gb[...].reshape(384, 512), preferred_element_type=F32).astype(BF16)

    dw_copy = pltpu.make_async_copy(dw, dw_hbm, local.at[1])
    dw_copy.start()

    lane = lax.broadcasted_iota(jnp.int32, (1, 128), 1)
    row_loss = jnp.zeros((1, 128), F32)
    for s in range(4):
        log_total = lt[s, 0:1, :]
        row_loss = row_loss + (log_total - lt[s, 1:2, :] + Z_WEIGHT * log_total * log_total)
    loss_out[0] = jnp.sum(jnp.where(lane < 48, row_loss, 0.0)) / MB_TOK
    loss_out[1] = jnp.sum(jnp.where((lane >= 48) & (lane < 96), row_loss, 0.0)) / MB_TOK

    for t in moves:
        t.wait_recv()
    acc = zs[3, pl.ds(zl * 4, 4)].astype(F32)
    for k in range(4):
        for n in range(0 if k else 1, 3):
            acc = acc + za[k, n].astype(F32)
        acc = acc + zb[k].reshape(4, 16, 384).astype(F32)
    zsum[...] = acc
    zq[...] = acc.astype(BF16)

    moves = [send(zq.at[lax.rem(zh + k, 4)], zr.at[k - 1], at(z=z + 4 * k)) for k in (2, 1, 3)]
    dw_copy.wait()
    wait_sends()
    for t in moves:
        t.wait_recv()
    pk[...] = zsum[zh] + zr[0].astype(F32) + zr[1].astype(F32) + zr[2].astype(F32)
    rows = []
    for i in range(3):
        rows.append(jnp.concatenate([pk[j : j + 1, i * 128 : (i + 1) * 128] for j in range(16)], axis=1))
    dh_out[...] = jnp.concatenate(rows, axis=0).astype(BF16)

    wait_sends()


FAR_FIRST = (8, 7, 9, 6, 10, 5, 11, 4, 12, 3, 13, 2, 14, 1, 15)
N_COPIES = 3 + 4 + 1 + 19 + 4 + 12 + 7 + 3 + 3 + 15 + 3 + 4 + 19 + 3


def on_device(hidden, head_weight, targets):
    vmem = pl.BlockSpec(memory_space=pltpu.VMEM)
    smem = pl.BlockSpec(memory_space=pltpu.SMEM)
    hbm = pl.BlockSpec(memory_space=pltpu.HBM)
    anywhere = pl.BlockSpec(memory_space=pl.ANY)
    scratch = [
        ((2048, 512), BF16),
        ((4, 96, 128), jnp.int32),
        ((4, 16, 16, 384), BF16),
        ((8, 48, 2048), BF16),
        ((8, 256, 384), BF16),
        ((4, 96, 512), F32),
        ((3, 4, 24, 512), F32),
        ((4, 24, 512), F32),
        ((8, 8, 128), F32),
        ((16, 8, 128), F32),
        ((4, 8, 128), F32),
        ((4, 8, 128), F32),
        ((4, 96, 512), BF16),
        ((4, 96, 512), BF16),
        ((4, 96, 512), BF16),
        ((4, 96, 128), F32),
        ((4, 2, 48, 2048), F32),
        ((4, 2, 48, 2048), F32),
        ((4, 48, 2048), BF16),
        ((4, 48, 2048), BF16),
        ((256, 384), BF16),
        ((4, 16, 16, 384), BF16),
        ((4, 3, 4, 16, 384), BF16),
        ((4, 2, 2, 16, 384), BF16),
        ((4, 16, 384), F32),
        ((4, 16, 384), BF16),
        ((3, 16, 384), BF16),
        ((2048, 512), BF16),
        ((16, 384), F32),
        ((4, 48, 2048), BF16),
        ((4, 48, 2048), BF16),
        ((2, 8, 128), F32),
    ]
    return pl.pallas_call(
        kernel,
        out_shape=(
            jax.ShapeDtypeStruct((3, 2048), BF16),
            jax.ShapeDtypeStruct((2048, 512), BF16),
            jax.ShapeDtypeStruct((2,), F32),
        ),
        in_specs=[vmem, hbm, smem],
        out_specs=(vmem, anywhere, smem),
        scratch_shapes=[pltpu.VMEM(s, t) for s, t in scratch]
        + [pltpu.SemaphoreType.DMA((N_COPIES,)), pltpu.SemaphoreType.DMA((N_COPIES,)), pltpu.SemaphoreType.DMA((2,))],
        compiler_params=pltpu.CompilerParams(
            collective_id=0, has_side_effects=True, vmem_limit_bytes=50 * 1024 * 1024
        ),
        name="head",
    )(hidden, head_weight, targets)


def solution(mesh):
    return jax.shard_map(
        on_device,
        mesh=mesh,
        in_specs=(P(("vocab", "rep"), "section"), P("section", ("vocab", "rep")), P()),
        out_specs=(P(("vocab", "rep"), "section"), P("section", ("vocab", "rep")), P()),
        check_vma=False,
    )
```
